512 devices in a mesh: band: 16 (over z_hi, y), grid: 32 (over z_lo, x, core).
Axes of the slice: x: 4, y: 4, z: 16 (z_hi: 4, z_lo: 4; z = z_hi * 4 + z_lo), core: 2. Of those that a mesh axis runs over, the one named last changes fastest.
Arguments:
- orbitals: bfloat16 [32, 160, 160, 160], P('band', 'grid'), may hold values from -6 to 6
- touched: int32 [2, 16], P(None, 'band'), may hold values from 0 to 1
Outputs:
- exchange_terms: float32 [32, 160, 160, 160], P('band', 'grid')
The draws below stay inside these ranges and needn't reach their ends.
All inputs are finite; a program needn't handle non-finite values.
Results may differ from the reference program's by a relative error of at most 0.0003.
Values may be sent and summed in bfloat16 or wider, within the bound.
A program may use at most 64 MiB of HBM per device.

```python
import jax
import jax.numpy as jnp
from jax import lax

NG = 160
NB = 2
ROUNDS = 2
GROUPS = 16
BANDS = 32


def draw_orbitals(key, part):
    key = jax.random.fold_in(key, 11)
    noise_key = jax.random.fold_in(key, 0)
    shape = (BANDS, NG, NG, NG)
    return jnp.clip(jax.random.normal(noise_key, shape, jnp.float32), -6.0, 6.0).astype(jnp.bfloat16)


def with_ends(entries, own_key, low, largest):
    place = [jax.random.randint(jax.random.fold_in(own_key, axis), (), 0, length) for axis, length in enumerate(entries.shape)]
    main_axis = entries.shape.index(max(entries.shape))
    beside = place[:main_axis] + [(place[main_axis] + 1) % entries.shape[main_axis]] + place[main_axis + 1:]
    return entries.at[tuple(place)].set(low).at[tuple(beside)].set(largest)


def setup_inputs(seed: int = 0) -> dict:
    key_of = jax.random.split(jax.random.key(seed), 3)
    orbitals = draw_orbitals(jax.random.fold_in(key_of[2], 71), 0)
    touched = with_ends(jax.random.randint(key_of[1], (ROUNDS, GROUPS), 0, NB), jax.random.fold_in(key_of[1], 1), 0, NB - 1).astype(jnp.int32)
    return dict(orbitals=orbitals, touched=touched)


def screened(length):
    wave = jnp.arange(length, dtype=jnp.int32)
    folded = jnp.minimum(wave, length - wave).astype(jnp.float32)
    halved = folded[: length // 2 + 1]
    square = folded[:, None, None] ** 2 + folded[None, :, None] ** 2 + halved[None, None, :] ** 2
    scaled = square / (0.0003 * length * length)
    safe = jnp.where(scaled > 0, scaled, 1.0)
    return 100.0 * jnp.where(scaled > 0, -jnp.expm1(-safe) / safe, 1.0)


def potential_of(density, factor):
    spectrum = jnp.fft.rfftn(density, axes=(-3, -2, -1))
    return jnp.fft.irfftn(factor * spectrum, s=density.shape[-3:], axes=(-3, -2, -1))


def reference(orbitals, touched):
    groups = touched.shape[1]
    own_count = orbitals.shape[0] // groups
    length = orbitals.shape[1]
    blocks = orbitals.reshape(groups, own_count, length, length, length)
    factor = screened(length)
    result = jnp.zeros(blocks.shape, jnp.float32)
    for step in range(2):
        offset = step + 1
        source = ((jnp.arange(groups, dtype=jnp.int32) - offset) % groups).astype(jnp.int32)
        picked = touched[step][source].astype(jnp.int32)
        visitor = blocks[source, picked]

        def per_group(pair):
            own_bands, guest = pair
            guest_wide = guest.astype(jnp.float32)
            own_wide = own_bands.astype(jnp.float32)

            def one_band(band):
                return potential_of(band * guest_wide, factor)

            potentials = lax.map(one_band, own_wide)
            return guest_wide[None] * potentials, jnp.sum(own_wide * potentials, axis=0)

        added, returned = lax.map(per_group, (blocks, visitor))
        result = result + added
        result = result.at[source, picked].add(returned)
    return result.reshape(orbitals.shape)
```

```python
import functools

import jax
import jax.numpy as jnp
import ml_dtypes
import numpy as np
from jax import lax
from jax.experimental import pallas as pl
from jax.experimental.pallas import tpu as pltpu
from jax.sharding import PartitionSpec as P

MESH = pl.DeviceIdType.MESH
F32, BF16, I16, I32 = jnp.float32, jnp.bfloat16, jnp.int16, jnp.int32

N = 160
G = 32
PL = 5
ROWS = 32
PACKED = 1008
CHUNK = ((0, 256), (256, 256), (512, 256), (768, 240))
FLOWS = ((0, 3, 0), (1, 2, 0), (1, 3, 1))
FULL = 32000.0


def split(x):
    hi = x.astype(BF16)
    return hi, (x - hi.astype(F32)).astype(BF16)


def dot(a, b):
    return jnp.dot(a, b, preferred_element_type=F32)


def dot_left(table, x):
    hi, lo = split(x)
    return dot(table[0], hi) + dot(table[0], lo) + dot(table[1], hi)


def dot_right(hi, lo, table):
    return dot(hi, table[0]) + dot(lo, table[0]) + dot(hi, table[1])


def exponent_of(largest):
    return jnp.ceil(8.0 * jnp.log2(jnp.maximum(largest, 1e-30)))


def step_up(e):
    return FULL * jnp.exp2(-0.125 * e)


def step_down(e):
    return jnp.exp2(0.125 * e) * (1.0 / FULL)


def iota(shape, axis):
    return lax.broadcasted_iota(I32, shape, axis)


def every(start, size):
    return pl.ds(start, size, stride=ROWS)


def to_i16(x):
    return x.astype(I32).astype(I16)


def kernel(
    orb, touched, ty, tyi, tx, txi, tz, tzi, out,
    lend, seen, vis, relay_f, ret, ret_send, ret_got, relay_b,
    c, send32, recv32, dhi, dlo, quant, grid_v,
    send_f, recv_f, send_b, recv_b,
    v_send, v_recv, vr_send, vr_recv, r_send, r_recv, rr_send, rr_recv,
    f_send, f_recv, b_send, b_recv,
):
    b, g = lax.axis_index("band"), lax.axis_index("grid")
    zh, y = b // 4, b % 4
    up, down = (zh + 1) % 4, (zh + 3) % 4
    lane32 = iota((G, 128), 1)
    group32 = lane32 // 32

    barrier = pltpu.get_barrier_semaphore()

    def greet_grid(i, _):
        pl.semaphore_signal(barrier, inc=1, device_id=(b, (g + i) % G), device_id_type=MESH)
        return 0

    for d in range(1, 4):
        pl.semaphore_signal(barrier, inc=1, device_id=(zh * 4 + (y + d) % 4, g), device_id_type=MESH)
    for block in (up, down):
        for yy in range(4):
            pl.semaphore_signal(barrier, inc=1, device_id=(block * 4 + yy, g), device_id_type=MESH)
    lax.fori_loop(1, G, greet_grid, 0)

    def pack(plane, store):
        tails = []
        for x in range(PL):
            v = plane(x)
            store(x * N, N, v[:, :128])
            tails.append(v[:, 128:N])
        store(PL * N, N, jnp.concatenate(tails[:4], axis=1))
        t = tails[4]
        rest = jnp.concatenate([t[144:160], jnp.zeros((32, 32), F32)], axis=0)
        return jnp.concatenate([t[0:48], t[48:96], t[96:144], rest], axis=1)

    def unpack(x, load):
        main = load(x * N, N)
        if x < 4:
            tail = load(PL * N, N)[:, 32 * x : 32 * x + 32]
        else:
            last = load(6 * N, 48)
            tail = jnp.concatenate(
                [last[:, 0:32], last[:, 32:64], last[:, 64:96], last[0:16, 96:128]], axis=0
            )
        return jnp.concatenate([main, tail], axis=1)

    for r in range(2):
        chosen = touched[r, 0]

        def lent(x, chosen=chosen):
            pick = jnp.full((N, N), chosen, I32) == 0
            return jnp.where(pick, orb[0, x].astype(F32), orb[1, x].astype(F32))

        def put(start, size, v, r=r):
            lend[r, start : start + size, :] = v.astype(BF16)

        put(6 * N, 48, pack(lent, put))

    pl.semaphore_wait(barrier, 42)

    def copy(src, dst, s, q, device):
        return pltpu.make_async_remote_copy(
            src_ref=src, dst_ref=dst, send_sem=s, recv_sem=q, device_id=device, device_id_type=MESH
        )

    def landed(ref, sem):
        pltpu.make_async_copy(ref, ref, sem).wait()

    def ship(r, forward, src, dst, s, q, relay, rs, rq):
        ahead = r + 1 if forward else -r - 1
        inside = y + ahead < 4 if forward else y + ahead >= 0
        block = up if forward else down

        @pl.when(inside)
        def _():
            copy(src.at[r], dst.at[r], s.at[r], q.at[r], (b + ahead, g)).start()

        for f, (fr, low, high) in enumerate(FLOWS):
            if fr != r:
                continue
            begin, end = (low, high) if forward else (high, low)

            @pl.when(y == begin)
            def _():
                for col, (start, size) in enumerate(CHUNK):
                    part = src.at[r, pl.ds(start, size)]
                    if col == begin:
                        goal = dst.at[r, pl.ds(start, size)]
                        copy(part, goal, s.at[r], q.at[r], (block * 4 + end, g)).start()
                    else:
                        goal = relay.at[f, pl.ds(0, size)]
                        copy(part, goal, s.at[r], rq.at[f], (zh * 4 + col, g)).start()

    def pass_on(r, forward, dst, q, relay, rs, rq):
        block = up if forward else down
        for f, (fr, low, high) in enumerate(FLOWS):
            if fr != r:
                continue
            begin, end = (low, high) if forward else (high, low)
            for col, (start, size) in enumerate(CHUNK):
                if col == begin:
                    continue

                @pl.when(y == col)
                def _():
                    part = relay.at[f, pl.ds(0, size)]
                    landed(part, rq.at[f])
                    goal = dst.at[r, pl.ds(start, size)]
                    copy(part, goal, rs.at[f], q.at[r], (block * 4 + end, g)).start()

    def shipped(forward, src, s, relay, rs):
        for r in range(2):
            landed(src.at[r], s.at[r])
        for f, (fr, low, high) in enumerate(FLOWS):
            begin = low if forward else high
            for col, (start, size) in enumerate(CHUNK):
                if col == begin:
                    continue

                @pl.when(y == col)
                def _():
                    landed(relay.at[f, pl.ds(0, size)], rs.at[f])

    for r in range(2):
        ship(r, True, lend, seen, v_send, v_recv, relay_f, vr_send, vr_recv)
    for r in range(2):
        pass_on(r, True, seen, v_recv, relay_f, vr_send, vr_recv)

    def fill(j, _):
        def squared(k):
            q = jnp.minimum(k, N - k).astype(F32)
            return q * q

        kz = jnp.minimum(iota((N, 256), 1), N)
        square = squared(iota((N, 256), 0)) + squared(kz)
        ky = 32 * j + g
        q2 = jnp.minimum(ky, N - ky).astype(F32)
        s = (square + q2 * q2) * (1.0 / (0.0003 * N * N))
        safe = jnp.where(s > 0, s, 1.0)
        factor = jnp.where(s > 0, (1.0 - jnp.exp(-safe)) / safe, 1.0)
        c[j] = factor * (100.0 / float(N) ** 3)
        return 0

    lax.fori_loop(0, PL, fill, 0)

    def see(r):
        landed(seen.at[r], v_recv.at[r])
        for x in range(PL):
            vis[r, x] = unpack(x, lambda start, size: seen[r, start : start + size, :].astype(F32))

    def send_all(a, src, dst, s, q):
        own = pl.ds(pl.multiple_of(g * ROWS, ROWS), ROWS)
        dst[a, own, :] = src[a, own, :]

        def start(i, _):
            p = (g + i) % G
            copy(
                src.at[a, pl.ds(pl.multiple_of(p * ROWS, ROWS), ROWS)],
                dst.at[a, own],
                s.at[a],
                q.at[a],
                (b, p),
            ).start()
            return 0

        lax.fori_loop(1, G, start, 0)

    def all_landed(a, ref, sem):
        part = ref.at[a, pl.ds(0, (G - 1) * ROWS)]
        pltpu.make_async_copy(part, part, sem.at[a]).wait()

    def stage_a(r, band):
        a = 2 * r + band

        def plane(x, carry):
            tail4, last = carry
            density = orb[band, x].astype(F32) * vis[r, x]
            spread = dot_left((ty[0], ty[1]), density)
            largest = jnp.max(jnp.abs(spread), axis=1, keepdims=True)
            e = exponent_of(largest)
            q = jnp.round(spread * step_up(e))
            tails = []
            for j in range(PL):
                part = q[32 * j : 32 * j + 32]
                send32[every(5 * x + j, G), :] = part[:, :128]
                tails.append(part[:, 128:N])
                last = jnp.where(lane32 == 32 + 5 * x + j, e[32 * j : 32 * j + 32], last)
            send32[every(25 + x, G), :] = jnp.concatenate(tails[:4], axis=1)
            spare = jnp.concatenate([tails[4]] * 4, axis=1)
            tail4 = jnp.where(group32 == x, spare, tail4)
            last = jnp.where(group32 + 4 == x, spare, last)
            return tail4, last

        zero = jnp.zeros((G, 128), F32)
        tail4, last = lax.fori_loop(0, PL, plane, (zero, zero))
        send32[every(30, G), :] = tail4
        send32[every(31, G), :] = last
        send_f[a] = to_i16(send32[...])
        send_all(a, send_f, recv_f, f_send, f_recv)

    def scales():
        return step_down(recv32[every(31, G), :])

    def scale_of(down_by, x, j):
        at = 32 + 5 * x + j
        return down_by[:, at : at + 1]

    def last_tail(x):
        if x == 4:
            return recv32[every(31, G), :]
        t = recv32[every(30, G), :]
        return pltpu.roll(t, 128 - 32 * x, 1) if x else t

    def stage_b(a):
        all_landed(a, recv_f, f_recv)
        recv32[...] = recv_f[a].astype(F32)
        down_by = scales()
        for x in range(PL):
            rows = slice(32 * x, 32 * x + 32)
            by = [scale_of(down_by, x, j) for j in range(PL)]
            mixed = jnp.where(
                group32 == 0, by[0], jnp.where(group32 == 1, by[1], jnp.where(group32 == 2, by[2], by[3]))
            )
            t_hi, t_lo = split(recv32[every(25 + x, G), :] * mixed)
            for j in range(PL):
                hi, lo = split(recv32[every(5 * x + j, G), :] * by[j])
                dhi[j, rows, :128] = hi
                dlo[j, rows, :128] = lo
                if j == 4:
                    t_hi, t_lo = split(last_tail(x) * by[4])
                dhi[j, rows, 128:] = t_hi
                dlo[j, rows, 128:] = t_lo

        def row(j, last):
            v = j % 4
            z = dot_right(dhi[j], dlo[j], (tz[0, v], tz[1, v]))
            w = dot_left((tx[0], tx[1]), z) * c[j]
            u = dot_left((txi[0], txi[1]), w)
            hi, lo = split(u)
            o = dot_right(hi, lo, (tzi[0, v], tzi[1, v]))
            e = exponent_of(jnp.max(jnp.abs(o), axis=1, keepdims=True))
            quant[j] = jnp.round(o * step_up(e))
            for x in range(PL):
                last = jnp.where(lane32 == 32 + 5 * x + j, e[32 * x : 32 * x + 32], last)
            return last

        last = lax.fori_loop(0, PL, row, jnp.zeros((G, 128), F32))
        tail4 = jnp.zeros((G, 128), F32)
        for x in range(PL):
            rows = slice(32 * x, 32 * x + 32)
            for j in range(PL):
                send32[every(5 * x + j, G), :] = quant[j, rows, :128]
            send32[every(25 + x, G), :] = (
                quant[0, rows, 128:] + quant[1, rows, 128:] + quant[2, rows, 128:] + quant[3, rows, 128:]
            )
            t = quant[4, rows, 128:]
            if x == 4:
                last = last + t
            else:
                tail4 = tail4 + (pltpu.roll(t, 32 * x, 1) if x else t)
        send32[every(30, G), :] = tail4
        send32[every(31, G), :] = last
        send_b[a] = to_i16(send32[...])
        send_all(a, send_b, recv_b, b_send, b_recv)

    def stage_c(r, band):
        a = 2 * r + band
        all_landed(a, recv_b, b_recv)
        recv32[...] = recv_b[a].astype(F32)
        down_by = scales()
        for x in range(PL):
            t = recv32[every(25 + x, G), :]
            for j in range(PL):
                rows = slice(32 * j, 32 * j + 32)
                by = scale_of(down_by, x, j)
                grid_v[x, rows, :128] = recv32[every(5 * x + j, G), :] * by
                if j == 4:
                    tail = last_tail(x)
                else:
                    tail = pltpu.roll(t, 128 - 32 * j, 1) if j else t
                grid_v[x, rows, 128:] = tail * by

        def plane(x, _):
            potential = dot_left((tyi[0], tyi[1]), grid_v[x])[:, :N]
            added = vis[r, x] * potential
            back = orb[band, x].astype(F32) * potential
            out[band, x] = added if r == 0 else out[band, x] + added
            ret[x] = back if band == 0 else ret[x] + back
            return 0

        lax.fori_loop(0, PL, plane, 0)

    def give_back(r):
        exps = []

        def scaled(x):
            v = ret[x]
            largest = jnp.max(jnp.max(jnp.abs(v), axis=1, keepdims=True), axis=0, keepdims=True)
            e = exponent_of(largest)
            exps.append(e)
            return jnp.round(v * step_up(e))

        def put(start, size, v):
            ret_send[r, start : start + size, :] = to_i16(v)

        last = pack(scaled, put)
        free = iota((48, 128), 0) >= 16
        lane = iota((48, 128), 1)
        for x in range(PL):
            last = jnp.where(free & (lane == 96 + x), exps[x], last)
        put(6 * N, 48, last)
        ship(r, False, ret_send, ret_got, r_send, r_recv, relay_b, rr_send, rr_recv)

    def take_back(r):
        landed(ret_got.at[r], r_recv.at[r])
        chosen = touched[r, 0]
        tail = step_down(ret_got[r, 6 * N : 6 * N + 48, :].astype(F32)[16:24])
        for x in range(PL):
            by = tail[0:1, 96 + x : 97 + x]
            v = unpack(x, lambda start, size: ret_got[r, start : start + size, :].astype(F32)) * by
            mine = jnp.full((N, N), chosen, I32) == 0
            out[0, x] = out[0, x] + jnp.where(mine, v, 0.0)
            out[1, x] = out[1, x] + jnp.where(mine, 0.0, v)

    see(0)
    stage_a(0, 0)
    stage_a(0, 1)
    see(1)
    stage_a(1, 0)
    stage_a(1, 1)
    for a in range(4):
        stage_b(a)
    stage_c(0, 0)
    stage_c(0, 1)
    give_back(0)
    stage_c(1, 0)
    stage_c(1, 1)
    give_back(1)
    for r in range(2):
        pass_on(r, False, ret_got, r_recv, relay_b, rr_send, rr_recv)
    for r in range(2):
        take_back(r)
    for a in range(4):
        all_landed(a, send_f, f_send)
        all_landed(a, send_b, b_send)
    shipped(True, lend, v_send, relay_f, vr_send)
    shipped(False, ret_send, r_send, relay_b, rr_send)


def pair(table):
    hi = table.astype(ml_dtypes.bfloat16)
    lo = (table - hi.astype(np.float64)).astype(ml_dtypes.bfloat16)
    return np.stack([hi, lo])


def tables():
    k = np.arange(N)
    phase = (k[:, None] * k[None, :] % N) * (2.0 * np.pi / N)
    cas = np.cos(phase) + np.sin(phase)
    by_plane = (5 * np.arange(G)[None, :] + np.arange(PL)[:, None]).reshape(-1)
    ty = cas
    tx = cas[:, by_plane]
    tz = np.zeros((4, 256, 256))
    tzi = np.zeros((4, 256, 256))
    for v in range(4):
        at = 128 + 32 * v
        tz[v, :128, :N] = cas[:128]
        tz[v, at : at + 32, :N] = cas[128:]
        tzi[v, :N, :128] = cas[:, :128]
        tzi[v, :N, at : at + 32] = cas[:, 128:]
    return [pair(t) for t in (ty, ty.T, tx, tx.T, tz, tzi)]


def on_device(orbitals, touched):
    vmem, smem = pl.BlockSpec(memory_space=pltpu.VMEM), pl.BlockSpec(memory_space=pltpu.SMEM)
    dma = pltpu.SemaphoreType.DMA
    message = (4, G * ROWS, 128)
    return pl.pallas_call(
        kernel,
        out_shape=jax.ShapeDtypeStruct((2, PL, N, N), F32),
        in_specs=[vmem, smem] + [vmem] * 6,
        out_specs=vmem,
        scratch_shapes=[
            pltpu.VMEM((2, PACKED, 128), BF16),
            pltpu.VMEM((2, PACKED, 128), BF16),
            pltpu.VMEM((2, PL, N, N), F32),
            pltpu.VMEM((3, 256, 128), BF16),
            pltpu.VMEM((PL, N, N), F32),
            pltpu.VMEM((2, PACKED, 128), I16),
            pltpu.VMEM((2, PACKED, 128), I16),
            pltpu.VMEM((3, 256, 128), I16),
            pltpu.VMEM((PL, N, 256), F32),
            pltpu.VMEM((G * ROWS, 128), F32),
            pltpu.VMEM((G * ROWS, 128), F32),
            pltpu.VMEM((PL, N, 256), BF16),
            pltpu.VMEM((PL, N, 256), BF16),
            pltpu.VMEM((PL, N, 256), F32),
            pltpu.VMEM((PL, N, 256), F32),
            pltpu.VMEM(message, I16),
            pltpu.VMEM(message, I16),
            pltpu.VMEM(message, I16),
            pltpu.VMEM(message, I16),
            dma((2,)), dma((2,)), dma((3,)), dma((3,)),
            dma((2,)), dma((2,)), dma((3,)), dma((3,)),
            dma((4,)), dma((4,)), dma((4,)), dma((4,)),
        ],
        compiler_params=pltpu.CompilerParams(
            collective_id=0, has_side_effects=True, vmem_limit_bytes=44 << 20
        ),
        name="exchange",
    )(orbitals, touched, *[jnp.asarray(t) for t in tables()])


def solution(mesh):
    in_specs = (P("band", "grid", None, None), P(None, "band"))
    out_specs = P("band", "grid", None, None)
    return jax.shard_map(
        on_device, mesh=mesh, in_specs=in_specs, out_specs=out_specs, check_vma=False
    )
```

```python
import functools

import jax
import jax.numpy as jnp
import ml_dtypes
import numpy as np
from jax import lax
from jax.experimental import pallas as pl
from jax.experimental.pallas import tpu as pltpu
from jax.sharding import PartitionSpec as P

MESH = pl.DeviceIdType.MESH
F32, BF16, I16, I32 = jnp.float32, jnp.bfloat16, jnp.int16, jnp.int32

N = 160
G = 32
PL = 5
ROWS = 32
PACKED = 1008
FLOWS = ((0, 3, 0), (1, 2, 0), (1, 3, 1))
COLUMNS = ((0, 0, 256), (1, 256, 256), (2, 512, 256), (3, 768, 240))
MOST = 256
FULL = 32000.0


def split(x):
    hi = x.astype(BF16)
    return hi, (x - hi.astype(F32)).astype(BF16)


def dot(a, b):
    return jnp.dot(a, b, preferred_element_type=F32)


def stack(x, axis):
    hi, lo = split(x)
    return jnp.concatenate([hi, lo, hi], axis=axis)


def exponent_of(largest):
    return jnp.ceil(8.0 * jnp.log2(jnp.maximum(largest, 1e-30)))


def step_up(e):
    return FULL * jnp.exp2(-0.125 * e)


def step_down(e):
    return jnp.exp2(0.125 * e) * (1.0 / FULL)


def iota(shape, axis):
    return lax.broadcasted_iota(I32, shape, axis)


def every(start, size):
    return pl.ds(start, size, stride=ROWS)


def to_i16(x):
    return x.astype(I32).astype(I16)


def kernel(
    orb_h, touched_h, ty_h, tx_h, txi_h, tz_h, tzi_h, out,
    orb, touched, ty, tx, txi, tz, tzi, here,
    lend, seen, vis, relay_f, ret, ret_send, ret_got, relay_b,
    c, send32, recv32, left, above, quant, grid_v,
    send_f, recv_f, send_b, recv_b,
    v_send, v_recv, vr_send, vr_recv, r_send, r_recv, rr_send, rr_recv,
    f_send, f_recv, b_send, b_recv,
):
    b, g = lax.axis_index("band"), lax.axis_index("grid")
    zh, y = b // 4, b % 4
    up, down = (zh + 1) % 4, (zh + 3) % 4
    lane32 = iota((G, 128), 1)
    group32 = lane32 // 32

    loads = [
        pltpu.make_async_copy(src, dst, here.at[i])
        for i, (src, dst) in enumerate(
            zip((orb_h, ty_h, tx_h, txi_h, tz_h, tzi_h, touched_h), (orb, ty, tx, txi, tz, tzi, touched))
        )
    ]
    for load in loads:
        load.start()

    barrier = pltpu.get_barrier_semaphore()

    def greet_grid(i, _):
        pl.semaphore_signal(barrier, inc=1, device_id=(b, (g + i) % G), device_id_type=MESH)
        return 0

    for block in (up, down):
        for yy in range(4):
            pl.semaphore_signal(barrier, inc=1, device_id=(block * 4 + yy, g), device_id_type=MESH)
    for d in range(1, 4):
        pl.semaphore_signal(barrier, inc=1, device_id=(zh * 4 + (y + d) % 4, g), device_id_type=MESH)
    lax.fori_loop(1, G, greet_grid, 0)

    def pack(plane, store):
        tails = []
        for x in range(PL):
            v = plane(x)
            store(x * N, N, v[:, :128])
            tails.append(v[:, 128:N])
        store(PL * N, N, jnp.concatenate(tails[:4], axis=1))
        t = tails[4]
        rest = jnp.concatenate([t[144:160], jnp.zeros((32, 32), F32)], axis=0)
        return jnp.concatenate([t[0:48], t[48:96], t[96:144], rest], axis=1)

    def unpack(x, load):
        main = load(x * N, N)
        if x < 4:
            tail = load(PL * N, N)[:, 32 * x : 32 * x + 32]
        else:
            last = load(6 * N, 48)
            tail = jnp.concatenate(
                [last[:, 0:32], last[:, 32:64], last[:, 64:96], last[0:16, 96:128]], axis=0
            )
        return jnp.concatenate([main, tail], axis=1)

    loads[0].wait()
    loads[6].wait()
    for r in range(2):
        chosen = touched[0, r]

        def lent(x, chosen=chosen):
            pick = jnp.full((N, N), chosen, I32) == 0
            return jnp.where(pick, orb[0, x].astype(F32), orb[1, x].astype(F32))

        def put(start, size, v, r=r):
            lend[r, start : start + size, :] = v.astype(BF16)

        put(6 * N, 48, pack(lent, put))


    pl.semaphore_wait(barrier, 42)

    def copy(src, dst, s, q, device):
        return pltpu.make_async_remote_copy(
            src_ref=src, dst_ref=dst, send_sem=s, recv_sem=q, device_id=device, device_id_type=MESH
        )

    def landed(ref, sem):
        pltpu.make_async_copy(ref, ref, sem).wait()

    def crossing(r, forward):
        for f, (fr, low, high) in enumerate(FLOWS):
            if fr == r:
                yield f, *((low, high) if forward else (high, low)), COLUMNS

    def ship(r, forward, src, dst, s, q, relay, rq):
        ahead = r + 1 if forward else -r - 1
        inside = y + ahead < 4 if forward else y + ahead >= 0
        block = up if forward else down

        @pl.when(inside)
        def _():
            copy(src.at[r], dst.at[r], s.at[r], q.at[r], (b + ahead, g)).start()

        for f, begin, end, columns in crossing(r, forward):

            @pl.when(y == begin)
            def _():
                for col, start, size in columns:
                    part = src.at[r, pl.ds(start, size)]
                    if col == begin:
                        goal = dst.at[r, pl.ds(start, size)]
                        copy(part, goal, s.at[r], q.at[r], (block * 4 + end, g)).start()
                    else:
                        goal = relay.at[f, pl.ds(0, size)]
                        copy(part, goal, s.at[r], rq.at[f], (zh * 4 + col, g)).start()

    def relays(r, forward, relay, act):
        for f, begin, end, columns in crossing(r, forward):
            for col, start, size in columns:
                if col != begin:
                    pl.when(y == col)(
                        functools.partial(act, f, end, relay.at[f, pl.ds(0, size)], pl.ds(start, size))
                    )

    def pass_on(r, forward, dst, q, relay, rs, rq):
        block = up if forward else down

        def act(f, end, part, rows):
            landed(part, rq.at[f])
            copy(part, dst.at[r, rows], rs.at[f], q.at[r], (block * 4 + end, g)).start()

        relays(r, forward, relay, act)

    def passed(r, forward, relay, rs):
        relays(r, forward, relay, lambda f, end, part, rows: landed(part, rs.at[f]))

    def shipped(src, s):
        for r in range(2):
            landed(src.at[r], s.at[r])

    for r in range(2):
        ship(r, True, lend, seen, v_send, v_recv, relay_f, vr_recv)
    for r in range(2):
        pass_on(r, True, seen, v_recv, relay_f, vr_send, vr_recv)

    def fill(j, _):
        def squared(k):
            q = jnp.minimum(k, N - k).astype(F32)
            return q * q

        kz = jnp.minimum(iota((N, 256), 1), N)
        square = squared(iota((N, 256), 0)) + squared(kz)
        ky = 32 * j + g
        q2 = jnp.minimum(ky, N - ky).astype(F32)
        s = (square + q2 * q2) * (1.0 / (0.0003 * N * N))
        safe = jnp.where(s > 0, s, 1.0)
        factor = jnp.where(s > 0, (1.0 - jnp.exp(-safe)) / safe, 1.0)
        c[j] = factor * (100.0 / float(N) ** 3)
        return 0

    def see(r):
        landed(seen.at[r], v_recv.at[r])
        for x in range(PL):
            vis[r, x] = unpack(x, lambda start, size: seen[r, start : start + size, :].astype(F32))

    def send_all(a, src, dst, s, q):
        own = pl.ds(pl.multiple_of(g * ROWS, ROWS), ROWS)
        dst[a, own, :] = src[a, own, :]

        def start(i, _):
            p = (g + i) % G
            copy(
                src.at[a, pl.ds(pl.multiple_of(p * ROWS, ROWS), ROWS)],
                dst.at[a, own],
                s.at[a],
                q.at[a],
                (b, p),
            ).start()
            return 0

        lax.fori_loop(1, G, start, 0)

    def all_landed(a, ref, sem):
        part = ref.at[a, pl.ds(0, (G - 1) * ROWS)]
        pltpu.make_async_copy(part, part, sem.at[a]).wait()

    def stage_a(r, band):
        a = 2 * r + band

        def plane(x, carry):
            tail4, last = carry
            density = orb[band, x].astype(F32) * vis[r, x]
            spread = dot(ty[...], stack(density, 0))
            largest = jnp.max(jnp.abs(spread), axis=1, keepdims=True)
            e = exponent_of(largest)
            q = jnp.round(spread * step_up(e))
            tails = []
            for j in range(PL):
                part = q[32 * j : 32 * j + 32]
                send32[every(5 * x + j, G), :] = part[:, :128]
                tails.append(part[:, 128:N])
                last = jnp.where(lane32 == 32 + 5 * x + j, e[32 * j : 32 * j + 32], last)
            send32[every(25 + x, G), :] = jnp.concatenate(tails[:4], axis=1)
            spare = jnp.concatenate([tails[4]] * 4, axis=1)
            tail4 = jnp.where(group32 == x, spare, tail4)
            last = jnp.where(group32 + 4 == x, spare, last)
            return tail4, last

        zero = jnp.zeros((G, 128), F32)
        tail4, last = lax.fori_loop(0, PL, plane, (zero, zero), unroll=True)
        send32[every(30, G), :] = tail4
        send32[every(31, G), :] = last
        send_f[a] = to_i16(send32[...])
        send_all(a, send_f, recv_f, f_send, f_recv)

    def scales():
        return step_down(recv32[every(31, G), :])

    def scale_of(down_by, x, j):
        at = 32 + 5 * x + j
        return down_by[:, at : at + 1]

    def last_tail(x):
        if x == 4:
            return recv32[every(31, G), :]
        t = recv32[every(30, G), :]
        return pltpu.roll(t, 128 - 32 * x, 1) if x else t

    def stage_b(a):
        all_landed(a, recv_f, f_recv)
        recv32[...] = recv_f[a].astype(F32)
        down_by = scales()
        for x in range(PL):
            rows = slice(32 * x, 32 * x + 32)
            by = [scale_of(down_by, x, j) for j in range(PL)]
            mixed = jnp.where(
                group32 == 0, by[0], jnp.where(group32 == 1, by[1], jnp.where(group32 == 2, by[2], by[3]))
            )
            tail = split(recv32[every(25 + x, G), :] * mixed)
            for j in range(PL):
                main = split(recv32[every(5 * x + j, G), :] * by[j])
                if j == 4:
                    tail = split(last_tail(x) * by[4])
                for piece in range(3):
                    at = 256 * piece
                    left[j, rows, at : at + 128] = main[piece % 2]
                    left[j, rows, at + 128 : at + 256] = tail[piece % 2]

        for j in range(PL):
            above[j] = stack(dot(left[j], tz[j % 4]), 0)
        for j in range(PL):
            above[j] = stack(dot(tx[...], above[j]) * c[j], 0)
        for j in range(PL):
            left[j] = stack(dot(txi[...], above[j]), 1)
        last = jnp.zeros((G, 128), F32)
        for j in range(PL):
            o = dot(left[j], tzi[j % 4])
            e = exponent_of(jnp.max(jnp.abs(o), axis=1, keepdims=True))
            quant[j] = jnp.round(o * step_up(e))
            for x in range(PL):
                last = jnp.where(lane32 == 32 + 5 * x + j, e[32 * x : 32 * x + 32], last)
        tail4 = jnp.zeros((G, 128), F32)
        for x in range(PL):
            rows = slice(32 * x, 32 * x + 32)
            for j in range(PL):
                send32[every(5 * x + j, G), :] = quant[j, rows, :128]
            send32[every(25 + x, G), :] = (
                quant[0, rows, 128:] + quant[1, rows, 128:] + quant[2, rows, 128:] + quant[3, rows, 128:]
            )
            t = quant[4, rows, 128:]
            if x == 4:
                last = last + t
            else:
                tail4 = tail4 + (pltpu.roll(t, 32 * x, 1) if x else t)
        send32[every(30, G), :] = tail4
        send32[every(31, G), :] = last
        send_b[a] = to_i16(send32[...])
        send_all(a, send_b, recv_b, b_send, b_recv)

    def stage_c(r, band):
        a = 2 * r + band
        all_landed(a, recv_b, b_recv)
        recv32[...] = recv_b[a].astype(F32)
        down_by = scales()
        for x in range(PL):
            t = recv32[every(25 + x, G), :]
            for j in range(PL):
                rows = slice(32 * j, 32 * j + 32)
                by = scale_of(down_by, x, j)
                grid_v[x, rows, :128] = recv32[every(5 * x + j, G), :] * by
                if j == 4:
                    tail = last_tail(x)
                else:
                    tail = pltpu.roll(t, 128 - 32 * j, 1) if j else t
                grid_v[x, rows, 128:] = tail * by

        def plane(x, _):
            potential = dot(ty[...], stack(grid_v[x], 0))[:, :N]
            added = vis[r, x] * potential
            back = orb[band, x].astype(F32) * potential
            out[band, x] = added if r == 0 else out[band, x] + added
            ret[x] = back if band == 0 else ret[x] + back
            return 0

        lax.fori_loop(0, PL, plane, 0, unroll=True)

    def give_back(r):
        exps = []

        def scaled(x):
            v = ret[x]
            largest = jnp.max(jnp.max(jnp.abs(v), axis=1, keepdims=True), axis=0, keepdims=True)
            e = exponent_of(largest)
            exps.append(e)
            return jnp.round(v * step_up(e))

        def put(start, size, v):
            ret_send[r, start : start + size, :] = to_i16(v)

        last = pack(scaled, put)
        free = iota((48, 128), 0) >= 16
        lane = iota((48, 128), 1)
        for x in range(PL):
            last = jnp.where(free & (lane == 96 + x), exps[x], last)
        put(6 * N, 48, last)
        ship(r, False, ret_send, ret_got, r_send, r_recv, relay_b, rr_recv)

    def take_back(r):
        landed(ret_got.at[r], r_recv.at[r])
        chosen = touched[0, r]
        tail = step_down(ret_got[r, 6 * N : 6 * N + 48, :].astype(F32)[16:24])
        for x in range(PL):
            by = tail[0:1, 96 + x : 97 + x]
            v = unpack(x, lambda start, size: ret_got[r, start : start + size, :].astype(F32)) * by
            mine = jnp.full((N, N), chosen, I32) == 0
            out[0, x] = out[0, x] + jnp.where(mine, v, 0.0)
            out[1, x] = out[1, x] + jnp.where(mine, 0.0, v)

    loads[1].wait()
    see(0)
    stage_a(0, 0)
    stage_a(0, 1)
    for load in loads[2:6]:
        load.wait()
    lax.fori_loop(0, PL, fill, 0)
    see(1)
    stage_a(1, 0)
    stage_a(1, 1)

    def slab(i, _):
        stage_b(i)
        return 0

    lax.fori_loop(0, 4, slab, 0)
    stage_c(0, 0)
    stage_c(0, 1)
    give_back(0)
    stage_c(1, 0)
    stage_c(1, 1)
    give_back(1)
    for r in range(2):
        pass_on(r, False, ret_got, r_recv, relay_b, rr_send, rr_recv)
    for r in range(2):
        take_back(r)
    for a in range(4):
        all_landed(a, send_f, f_send)
        all_landed(a, send_b, b_send)
    shipped(lend, v_send)
    shipped(ret_send, r_send)
    for r in range(2):
        passed(r, True, relay_f, vr_send)
        passed(r, False, relay_b, rr_send)


def pieces(table, axis):
    hi = table.astype(ml_dtypes.bfloat16)
    lo = (table - hi.astype(np.float64)).astype(ml_dtypes.bfloat16)
    return np.concatenate([hi, hi, lo], axis=axis)


def tables():
    k = np.arange(N)
    phase = (k[:, None] * k[None, :] % N) * (2.0 * np.pi / N)
    cas = np.cos(phase) + np.sin(phase)
    by_plane = (5 * np.arange(G)[None, :] + np.arange(PL)[:, None]).reshape(-1)
    tx = cas[:, by_plane]
    tz = np.zeros((4, 256, 256))
    tzi = np.zeros((4, 256, 256))
    for v in range(4):
        at = 128 + 32 * v
        tz[v, :128, :N] = cas[:128]
        tz[v, at : at + 32, :N] = cas[128:]
        tzi[v, :N, :128] = cas[:, :128]
        tzi[v, :N, at : at + 32] = cas[:, 128:]
    left = [pieces(t, 1) for t in (cas, tx, tx.T)]
    return left + [pieces(t, 1) for t in (tz, tzi)]


def on_device(orbitals, touched):
    vmem = pl.BlockSpec(memory_space=pltpu.VMEM)
    hbm = pl.BlockSpec(memory_space=pltpu.HBM)
    dma = pltpu.SemaphoreType.DMA
    message = (4, G * ROWS, 128)
    return pl.pallas_call(
        kernel,
        out_shape=jax.ShapeDtypeStruct((2, PL, N, N), F32),
        in_specs=[hbm] * 7,
        out_specs=vmem,
        scratch_shapes=[
            pltpu.VMEM((2, PL, N, N), BF16),
            pltpu.SMEM((1, 2), I32),
            pltpu.VMEM((N, 3 * N), BF16),
            pltpu.VMEM((N, 3 * N), BF16),
            pltpu.VMEM((N, 3 * N), BF16),
            pltpu.VMEM((4, 768, 256), BF16),
            pltpu.VMEM((4, 768, 256), BF16),
            dma((7,)),
            pltpu.VMEM((2, PACKED, 128), BF16),
            pltpu.VMEM((2, PACKED, 128), BF16),
            pltpu.VMEM((2, PL, N, N), F32),
            pltpu.VMEM((3, MOST, 128), BF16),
            pltpu.VMEM((PL, N, N), F32),
            pltpu.VMEM((2, PACKED, 128), I16),
            pltpu.VMEM((2, PACKED, 128), I16),
            pltpu.VMEM((3, MOST, 128), I16),
            pltpu.VMEM((PL, N, 256), F32),
            pltpu.VMEM((G * ROWS, 128), F32),
            pltpu.VMEM((G * ROWS, 128), F32),
            pltpu.VMEM((PL, N, 768), BF16),
            pltpu.VMEM((PL, 3 * N, 256), BF16),
            pltpu.VMEM((PL, N, 256), F32),
            pltpu.VMEM((PL, N, 256), F32),
            pltpu.VMEM(message, I16),
            pltpu.VMEM(message, I16),
            pltpu.VMEM(message, I16),
            pltpu.VMEM(message, I16),
            dma((2,)), dma((2,)), dma((3,)), dma((3,)),
            dma((2,)), dma((2,)), dma((3,)), dma((3,)),
            dma((4,)), dma((4,)), dma((4,)), dma((4,)),
        ],
        compiler_params=pltpu.CompilerParams(
            collective_id=0, has_side_effects=True, vmem_limit_bytes=60 << 20
        ),
        name="exchange",
    )(orbitals, touched.T, *[jnp.asarray(t) for t in tables()])


def solution(mesh):
    in_specs = (P("band", "grid", None, None), P(None, "band"))
    out_specs = P("band", "grid", None, None)
    return jax.shard_map(
        on_device, mesh=mesh, in_specs=in_specs, out_specs=out_specs, check_vma=False
    )
```

```python
import functools

import jax
import jax.numpy as jnp
import ml_dtypes
import numpy as np
from jax import lax
from jax.experimental import pallas as pl
from jax.experimental.pallas import tpu as pltpu
from jax.sharding import PartitionSpec as P

MESH = pl.DeviceIdType.MESH
F32, BF16, I16, I32 = jnp.float32, jnp.bfloat16, jnp.int16, jnp.int32

N = 160
G = 32
PL = 5
ROWS = 32
PACKED = 1008
FLOWS = ((0, 3, 0), (1, 2, 0), (1, 3, 1))
BITS, BIT = 2, 128
COLUMNS = tuple(
    (col, k, 256 * col + BIT * k, min(BIT, PACKED - 256 * col - BIT * k))
    for k in range(BITS)
    for col in range(4)
)
FULL = 32000.0


def split(x):
    hi = x.astype(BF16)
    return hi, (x - hi.astype(F32)).astype(BF16)


def dot(a, b):
    return jnp.dot(a, b, preferred_element_type=F32)


def stack(x, axis):
    hi, lo = split(x)
    return jnp.concatenate([hi, lo, hi], axis=axis)


def exponent_of(largest):
    return jnp.ceil(8.0 * jnp.log2(jnp.maximum(largest, 1e-30)))


def step_up(e):
    return FULL * jnp.exp2(-0.125 * e)


def step_down(e):
    return jnp.exp2(0.125 * e) * (1.0 / FULL)


def iota(shape, axis):
    return lax.broadcasted_iota(I32, shape, axis)


def every(start, size):
    return pl.ds(start, size, stride=ROWS)


def to_i16(x):
    return x.astype(I32).astype(I16)


def kernel(
    orb_h, touched_h, ty_h, tx_h, txi_h, tz_h, tzi_h, out,
    orb, touched, ty, tx, txi, tz, tzi, here,
    lend, seen, vis, relay_f, ret, ret_send, ret_got, relay_b,
    c, send32, recv32, left, above, quant, grid_v,
    send_f, recv_f, send_b, recv_b,
    v_send, v_recv, vr_send, vr_recv, r_send, r_recv, rr_send, rr_recv,
    f_send, f_recv, b_send, b_recv,
):
    b, g = lax.axis_index("band"), lax.axis_index("grid")
    zh, y = b // 4, b % 4
    up, down = (zh + 1) % 4, (zh + 3) % 4
    lane32 = iota((G, 128), 1)
    group32 = lane32 // 32

    loads = [
        pltpu.make_async_copy(src, dst, here.at[i])
        for i, (src, dst) in enumerate(
            zip((orb_h, ty_h, tx_h, txi_h, tz_h, tzi_h, touched_h), (orb, ty, tx, txi, tz, tzi, touched))
        )
    ]
    for load in loads:
        load.start()

    barrier = pltpu.get_barrier_semaphore()

    def greet_grid(i, _):
        pl.semaphore_signal(barrier, inc=1, device_id=(b, (g + i) % G), device_id_type=MESH)
        return 0

    for block in (up, down):
        for yy in range(4):
            pl.semaphore_signal(barrier, inc=1, device_id=(block * 4 + yy, g), device_id_type=MESH)
    for d in range(1, 4):
        pl.semaphore_signal(barrier, inc=1, device_id=(zh * 4 + (y + d) % 4, g), device_id_type=MESH)
    lax.fori_loop(1, G, greet_grid, 0)

    def pack(plane, store):
        tails = []
        for x in range(PL):
            v = plane(x)
            store(x * N, N, v[:, :128])
            tails.append(v[:, 128:N])
        store(PL * N, N, jnp.concatenate(tails[:4], axis=1))
        t = tails[4]
        rest = jnp.concatenate([t[144:160], jnp.zeros((32, 32), F32)], axis=0)
        return jnp.concatenate([t[0:48], t[48:96], t[96:144], rest], axis=1)

    def unpack(x, load):
        main = load(x * N, N)
        if x < 4:
            tail = load(PL * N, N)[:, 32 * x : 32 * x + 32]
        else:
            last = load(6 * N, 48)
            tail = jnp.concatenate(
                [last[:, 0:32], last[:, 32:64], last[:, 64:96], last[0:16, 96:128]], axis=0
            )
        return jnp.concatenate([main, tail], axis=1)

    loads[0].wait()
    loads[6].wait()
    for r in range(2):
        chosen = touched[0, r]

        def lent(x, chosen=chosen):
            pick = jnp.full((N, N), chosen, I32) == 0
            return jnp.where(pick, orb[0, x].astype(F32), orb[1, x].astype(F32))

        def put(start, size, v, r=r):
            lend[r, start : start + size, :] = v.astype(BF16)

        put(6 * N, 48, pack(lent, put))


    pl.semaphore_wait(barrier, 42)

    def copy(src, dst, s, q, device):
        return pltpu.make_async_remote_copy(
            src_ref=src, dst_ref=dst, send_sem=s, recv_sem=q, device_id=device, device_id_type=MESH
        )

    def landed(ref, sem):
        pltpu.make_async_copy(ref, ref, sem).wait()

    def crossing(r, forward):
        for f, (fr, low, high) in enumerate(FLOWS):
            if fr == r:
                yield f, *((low, high) if forward else (high, low)), COLUMNS

    def ship(r, forward, src, dst, s, q, relay, rq):
        ahead = r + 1 if forward else -r - 1
        inside = y + ahead < 4 if forward else y + ahead >= 0
        block = up if forward else down

        @pl.when(inside)
        def _():
            copy(src.at[r], dst.at[r], s.at[r], q.at[r], (b + ahead, g)).start()

        for f, begin, end, columns in crossing(r, forward):

            @pl.when(y == begin)
            def _():
                for col, k, start, size in columns:
                    part = src.at[r, pl.ds(start, size)]
                    if col == begin:
                        goal = dst.at[r, pl.ds(start, size)]
                        copy(part, goal, s.at[r], q.at[r], (block * 4 + end, g)).start()
                    else:
                        goal = relay.at[f, pl.ds(BIT * k, size)]
                        copy(part, goal, s.at[r], rq.at[BITS * f + k], (zh * 4 + col, g)).start()

    def relays(r, forward, relay, act):
        for f, begin, end, columns in crossing(r, forward):
            for col, k, start, size in columns:
                if col != begin:
                    pl.when(y == col)(
                        functools.partial(act, BITS * f + k, end, relay.at[f, pl.ds(BIT * k, size)], pl.ds(start, size))
                    )

    def pass_on(r, forward, dst, q, relay, rs, rq):
        block = up if forward else down

        def act(f, end, part, rows):
            landed(part, rq.at[f])
            copy(part, dst.at[r, rows], rs.at[f], q.at[r], (block * 4 + end, g)).start()

        relays(r, forward, relay, act)

    def passed(r, forward, relay, rs):
        relays(r, forward, relay, lambda f, end, part, rows: landed(part, rs.at[f]))

    def shipped(src, s):
        for r in range(2):
            landed(src.at[r], s.at[r])

    for r in range(2):
        ship(r, True, lend, seen, v_send, v_recv, relay_f, vr_recv)
    for r in range(2):
        pass_on(r, True, seen, v_recv, relay_f, vr_send, vr_recv)

    def fill(j, _):
        def squared(k):
            q = jnp.minimum(k, N - k).astype(F32)
            return q * q

        kz = jnp.minimum(iota((N, 256), 1), N)
        square = squared(iota((N, 256), 0)) + squared(kz)
        ky = 32 * j + g
        q2 = jnp.minimum(ky, N - ky).astype(F32)
        s = (square + q2 * q2) * (1.0 / (0.0003 * N * N))
        safe = jnp.where(s > 0, s, 1.0)
        factor = jnp.where(s > 0, (1.0 - jnp.exp(-safe)) / safe, 1.0)
        c[j] = factor * (100.0 / float(N) ** 3)
        return 0

    def see(r):
        landed(seen.at[r], v_recv.at[r])
        for x in range(PL):
            vis[r, x] = unpack(x, lambda start, size: seen[r, start : start + size, :].astype(F32))

    def send_all(a, src, dst, s, q):
        own = pl.ds(pl.multiple_of(g * ROWS, ROWS), ROWS)
        dst[a, own, :] = src[a, own, :]

        def start(i, _):
            p = (g + i) % G
            copy(
                src.at[a, pl.ds(pl.multiple_of(p * ROWS, ROWS), ROWS)],
                dst.at[a, own],
                s.at[a],
                q.at[a],
                (b, p),
            ).start()
            return 0

        lax.fori_loop(1, G, start, 0)

    def all_landed(a, ref, sem):
        part = ref.at[a, pl.ds(0, (G - 1) * ROWS)]
        pltpu.make_async_copy(part, part, sem.at[a]).wait()

    def stage_a(r, band):
        a = 2 * r + band

        def plane(x, carry):
            tail4, last = carry
            density = orb[band, x].astype(F32) * vis[r, x]
            spread = dot(ty[...], stack(density, 0))
            largest = jnp.max(jnp.abs(spread), axis=1, keepdims=True)
            e = exponent_of(largest)
            q = jnp.round(spread * step_up(e))
            tails = []
            for j in range(PL):
                part = q[32 * j : 32 * j + 32]
                send32[every(5 * x + j, G), :] = part[:, :128]
                tails.append(part[:, 128:N])
                last = jnp.where(lane32 == 32 + 5 * x + j, e[32 * j : 32 * j + 32], last)
            send32[every(25 + x, G), :] = jnp.concatenate(tails[:4], axis=1)
            spare = jnp.concatenate([tails[4]] * 4, axis=1)
            tail4 = jnp.where(group32 == x, spare, tail4)
            last = jnp.where(group32 + 4 == x, spare, last)
            return tail4, last

        zero = jnp.zeros((G, 128), F32)
        tail4, last = lax.fori_loop(0, PL, plane, (zero, zero), unroll=True)
        send32[every(30, G), :] = tail4
        send32[every(31, G), :] = last
        send_f[a] = to_i16(send32[...])
        send_all(a, send_f, recv_f, f_send, f_recv)

    def scales():
        return step_down(recv32[every(31, G), :])

    def scale_of(down_by, x, j):
        at = 32 + 5 * x + j
        return down_by[:, at : at + 1]

    def last_tail(x):
        if x == 4:
            return recv32[every(31, G), :]
        t = recv32[every(30, G), :]
        return pltpu.roll(t, 128 - 32 * x, 1) if x else t

    def stage_b(a):
        all_landed(a, recv_f, f_recv)
        recv32[...] = recv_f[a].astype(F32)
        down_by = scales()
        for x in range(PL):
            rows = slice(32 * x, 32 * x + 32)
            by = [scale_of(down_by, x, j) for j in range(PL)]
            mixed = jnp.where(
                group32 == 0, by[0], jnp.where(group32 == 1, by[1], jnp.where(group32 == 2, by[2], by[3]))
            )
            tail = split(recv32[every(25 + x, G), :] * mixed)
            for j in range(PL):
                main = split(recv32[every(5 * x + j, G), :] * by[j])
                if j == 4:
                    tail = split(last_tail(x) * by[4])
                for piece in range(3):
                    at = 256 * piece
                    left[j, rows, at : at + 128] = main[piece % 2]
                    left[j, rows, at + 128 : at + 256] = tail[piece % 2]

        for j in range(PL):
            above[j] = stack(dot(left[j], tz[j % 4]), 0)
        for j in range(PL):
            above[j] = stack(dot(tx[...], above[j]) * c[j], 0)
        for j in range(PL):
            left[j] = stack(dot(txi[...], above[j]), 1)
        last = jnp.zeros((G, 128), F32)
        for j in range(PL):
            o = dot(left[j], tzi[j % 4])
            e = exponent_of(jnp.max(jnp.abs(o), axis=1, keepdims=True))
            quant[j] = jnp.round(o * step_up(e))
            for x in range(PL):
                last = jnp.where(lane32 == 32 + 5 * x + j, e[32 * x : 32 * x + 32], last)
        tail4 = jnp.zeros((G, 128), F32)
        for x in range(PL):
            rows = slice(32 * x, 32 * x + 32)
            for j in range(PL):
                send32[every(5 * x + j, G), :] = quant[j, rows, :128]
            send32[every(25 + x, G), :] = (
                quant[0, rows, 128:] + quant[1, rows, 128:] + quant[2, rows, 128:] + quant[3, rows, 128:]
            )
            t = quant[4, rows, 128:]
            if x == 4:
                last = last + t
            else:
                tail4 = tail4 + (pltpu.roll(t, 32 * x, 1) if x else t)
        send32[every(30, G), :] = tail4
        send32[every(31, G), :] = last
        send_b[a] = to_i16(send32[...])
        send_all(a, send_b, recv_b, b_send, b_recv)

    def stage_c(r, band):
        a = 2 * r + band
        all_landed(a, recv_b, b_recv)
        recv32[...] = recv_b[a].astype(F32)
        down_by = scales()
        for x in range(PL):
            t = recv32[every(25 + x, G), :]
            for j in range(PL):
                rows = slice(32 * j, 32 * j + 32)
                by = scale_of(down_by, x, j)
                grid_v[x, rows, :128] = recv32[every(5 * x + j, G), :] * by
                if j == 4:
                    tail = last_tail(x)
                else:
                    tail = pltpu.roll(t, 128 - 32 * j, 1) if j else t
                grid_v[x, rows, 128:] = tail * by

        def plane(x, _):
            potential = dot(ty[...], stack(grid_v[x], 0))[:, :N]
            added = vis[r, x] * potential
            back = orb[band, x].astype(F32) * potential
            out[band, x] = added if r == 0 else out[band, x] + added
            ret[x] = back if band == 0 else ret[x] + back
            return 0

        lax.fori_loop(0, PL, plane, 0, unroll=True)

    def give_back(r):
        exps = []

        def scaled(x):
            v = ret[x]
            largest = jnp.max(jnp.max(jnp.abs(v), axis=1, keepdims=True), axis=0, keepdims=True)
            e = exponent_of(largest)
            exps.append(e)
            return jnp.round(v * step_up(e))

        def put(start, size, v):
            ret_send[r, start : start + size, :] = to_i16(v)

        last = pack(scaled, put)
        free = iota((48, 128), 0) >= 16
        lane = iota((48, 128), 1)
        for x in range(PL):
            last = jnp.where(free & (lane == 96 + x), exps[x], last)
        put(6 * N, 48, last)
        ship(r, False, ret_send, ret_got, r_send, r_recv, relay_b, rr_recv)

    def take_back(r):
        landed(ret_got.at[r], r_recv.at[r])
        chosen = touched[0, r]
        tail = step_down(ret_got[r, 6 * N : 6 * N + 48, :].astype(F32)[16:24])
        for x in range(PL):
            by = tail[0:1, 96 + x : 97 + x]
            v = unpack(x, lambda start, size: ret_got[r, start : start + size, :].astype(F32)) * by
            mine = jnp.full((N, N), chosen, I32) == 0
            out[0, x] = out[0, x] + jnp.where(mine, v, 0.0)
            out[1, x] = out[1, x] + jnp.where(mine, 0.0, v)

    loads[1].wait()
    see(0)
    stage_a(0, 0)
    stage_a(0, 1)
    for load in loads[2:6]:
        load.wait()
    lax.fori_loop(0, PL, fill, 0)
    see(1)
    stage_a(1, 0)
    stage_a(1, 1)

    def slab(i, _):
        stage_b(i)
        return 0

    lax.fori_loop(0, 4, slab, 0)
    stage_c(0, 0)
    stage_c(0, 1)
    give_back(0)
    stage_c(1, 0)
    stage_c(1, 1)
    give_back(1)
    for r in range(2):
        pass_on(r, False, ret_got, r_recv, relay_b, rr_send, rr_recv)
    for r in range(2):
        take_back(r)
    for a in range(4):
        all_landed(a, send_f, f_send)
        all_landed(a, send_b, b_send)
    shipped(lend, v_send)
    shipped(ret_send, r_send)
    for r in range(2):
        passed(r, True, relay_f, vr_send)
        passed(r, False, relay_b, rr_send)


def pieces(table, axis):
    hi = table.astype(ml_dtypes.bfloat16)
    lo = (table - hi.astype(np.float64)).astype(ml_dtypes.bfloat16)
    return np.concatenate([hi, hi, lo], axis=axis)


def tables():
    k = np.arange(N)
    phase = (k[:, None] * k[None, :] % N) * (2.0 * np.pi / N)
    cas = np.cos(phase) + np.sin(phase)
    by_plane = (5 * np.arange(G)[None, :] + np.arange(PL)[:, None]).reshape(-1)
    tx = cas[:, by_plane]
    tz = np.zeros((4, 256, 256))
    tzi = np.zeros((4, 256, 256))
    for v in range(4):
        at = 128 + 32 * v
        tz[v, :128, :N] = cas[:128]
        tz[v, at : at + 32, :N] = cas[128:]
        tzi[v, :N, :128] = cas[:, :128]
        tzi[v, :N, at : at + 32] = cas[:, 128:]
    left = [pieces(t, 1) for t in (cas, tx, tx.T)]
    return left + [pieces(t, 1) for t in (tz, tzi)]


def on_device(orbitals, touched):
    vmem = pl.BlockSpec(memory_space=pltpu.VMEM)
    hbm = pl.BlockSpec(memory_space=pltpu.HBM)
    dma = pltpu.SemaphoreType.DMA
    message = (4, G * ROWS, 128)
    return pl.pallas_call(
        kernel,
        out_shape=jax.ShapeDtypeStruct((2, PL, N, N), F32),
        in_specs=[hbm] * 7,
        out_specs=vmem,
        scratch_shapes=[
            pltpu.VMEM((2, PL, N, N), BF16),
            pltpu.SMEM((1, 2), I32),
            pltpu.VMEM((N, 3 * N), BF16),
            pltpu.VMEM((N, 3 * N), BF16),
            pltpu.VMEM((N, 3 * N), BF16),
            pltpu.VMEM((4, 768, 256), BF16),
            pltpu.VMEM((4, 768, 256), BF16),
            dma((7,)),
            pltpu.VMEM((2, PACKED, 128), BF16),
            pltpu.VMEM((2, PACKED, 128), BF16),
            pltpu.VMEM((2, PL, N, N), F32),
            pltpu.VMEM((3, BITS * BIT, 128), BF16),
            pltpu.VMEM((PL, N, N), F32),
            pltpu.VMEM((2, PACKED, 128), I16),
            pltpu.VMEM((2, PACKED, 128), I16),
            pltpu.VMEM((3, BITS * BIT, 128), I16),
            pltpu.VMEM((PL, N, 256), F32),
            pltpu.VMEM((G * ROWS, 128), F32),
            pltpu.VMEM((G * ROWS, 128), F32),
            pltpu.VMEM((PL, N, 768), BF16),
            pltpu.VMEM((PL, 3 * N, 256), BF16),
            pltpu.VMEM((PL, N, 256), F32),
            pltpu.VMEM((PL, N, 256), F32),
            pltpu.VMEM(message, I16),
            pltpu.VMEM(message, I16),
            pltpu.VMEM(message, I16),
            pltpu.VMEM(message, I16),
            dma((2,)), dma((2,)), dma((3 * BITS,)), dma((3 * BITS,)),
            dma((2,)), dma((2,)), dma((3 * BITS,)), dma((3 * BITS,)),
            dma((4,)), dma((4,)), dma((4,)), dma((4,)),
        ],
        compiler_params=pltpu.CompilerParams(
            collective_id=0, has_side_effects=True, vmem_limit_bytes=60 << 20
        ),
        name="exchange",
    )(orbitals, touched.T, *[jnp.asarray(t) for t in tables()])


def solution(mesh):
    in_specs = (P("band", "grid", None, None), P(None, "band"))
    out_specs = P("band", "grid", None, None)
    return jax.shard_map(
        on_device, mesh=mesh, in_specs=in_specs, out_specs=out_specs, check_vma=False
    )
```
